512 devices in a mesh: wall: 16 (over z_lo, core), tang: 32 (over z_hi, y, x).
Axes of the slice: x: 4, y: 4, z: 16 (z_hi: 2, z_lo: 8; z = z_hi * 8 + z_lo), core: 2. Of those that a mesh axis runs over, the one named last changes fastest.
Arguments:
- right_side: float32 [32, 64, 384], P('wall', 'tang'), may hold values from -6 to 6
- inverse_blocks: bfloat16 [32, 64, 384, 384], P('wall', 'tang'), as said below
- lower_blocks: bfloat16 [32, 64, 384, 384], P('wall', 'tang'), may hold values from -0.375 to 0.375
- upper_blocks: bfloat16 [32, 64, 384, 384], P('wall', 'tang'), may hold values from -0.375 to 0.375
- trace_map: bfloat16 [384, 384], replicated, may hold values from -0.3125 to 0.3125
- lift_map: bfloat16 [384, 384], replicated, may hold values from -0.3125 to 0.3125
- neighbours: int32 [64, 4], P('tang'), may hold values from 0 to 63, as said below
Outputs:
- correction: float32 [32, 64, 384], P('wall', 'tang')
- face_residual: float32 [32, 64, 384], P('wall', 'tang')
The draws below stay inside these ranges and needn't reach their ends.
Inputs may be any that keep to these rules, and one draw needn't show every extreme that they name: `inverse_blocks`: given inverses of the factorization's diagonal blocks; entries of order one or less, every block of full rank. Face pairs are symmetric: neighbours[neighbours[l, 0], 1] = l and neighbours[neighbours[l, 2], 3] = l. Lines being split in order over tang, the line across face 0 or 2 lies at the same index of tang or the next one (cyclically), and the line across face 1 or 3 lies at the same index or the previous one.
All inputs are finite; a program needn't handle non-finite values.
Results may differ from the reference program's by a relative error of at most 0.0003.
Values sent between devices are 32-bit elements; how exact they have to be, the bound alone decides.
No kernel may reach another device: no remote copies, remote signals or barrier semaphores. Data moves between devices by JAX's collectives and lax.ppermute only.
A program may use at most 128 MiB of HBM per device.

```python
import jax
import jax.numpy as jnp
from jax import lax

LINES_DEV = 2
BLOCK = 384
TRACES = 384
NCELL = 32
LINES = 64


def draw_inverse_blocks(key, part):
    shape = (NCELL, LINES, BLOCK, BLOCK)
    rough = jax.random.normal(key, shape, jnp.float32) * (0.3 / BLOCK ** 0.5)
    return (rough + 0.6 * jnp.eye(BLOCK, dtype=jnp.float32)).astype(jnp.bfloat16)


def strip_order(key):
    groups = LINES // LINES_DEV
    keys = jax.random.split(key, groups)
    local = jax.vmap(lambda k: jax.random.permutation(k, LINES_DEV))(keys)
    order = (jnp.arange(groups, dtype=jnp.int32)[:, None] * LINES_DEV + local.astype(jnp.int32)).reshape(-1)
    following = jnp.roll(order, -1)
    preceding = jnp.roll(order, 1)
    ahead = jnp.zeros((LINES,), jnp.int32).at[order].set(following)
    behind = jnp.zeros((LINES,), jnp.int32).at[order].set(preceding)
    return (ahead, behind)


def draw_neighbours(key, part):
    first_ahead, first_behind = strip_order(jax.random.fold_in(key, 11))
    second_ahead, second_behind = strip_order(jax.random.fold_in(key, 23))
    return jnp.stack([first_ahead, first_behind, second_ahead, second_behind], axis=1).astype(jnp.int32)


def levels(rng, extent, cuts, smallest, largest):
    factor_of = 1.0
    for axis_at, blocks in cuts:
        draws = jax.random.uniform(jax.random.fold_in(jax.random.fold_in(rng, 6), axis_at), (blocks,), jnp.float32, smallest / len(cuts), largest / len(cuts))
        factor_of = factor_of * jnp.repeat(jnp.exp(draws), extent[axis_at] // blocks).reshape((-1,) + (1,) * (len(extent) - 1 - axis_at))
    return factor_of


def bell_draw(own_key, shape, scale, reach, cuts=(), kind=jnp.bfloat16):
    factor_of = levels(own_key, shape, cuts, -0.22, 0.18) if cuts else 1.0
    entries = jax.random.normal(own_key, shape, jnp.float32) * scale * factor_of
    return jnp.minimum(jnp.maximum(entries, -reach), reach).astype(kind)


def setup_inputs(seed: int = 0) -> dict:
    seeds = jax.random.split(jax.random.key(seed), 8)
    return {
        "right_side": bell_draw(seeds[0], (NCELL, LINES, BLOCK), 1.0, 6.0, ((0, 16), (1, 32)), jnp.float32),
        "inverse_blocks": draw_inverse_blocks(jax.random.fold_in(seeds[7], 71), 0),
        "lower_blocks": bell_draw(seeds[2], (NCELL, LINES, BLOCK, BLOCK), (BLOCK * 10 // 17) ** -0.5, 0.375, ((0, 16), (1, 32))),
        "upper_blocks": bell_draw(seeds[3], (NCELL, LINES, BLOCK, BLOCK), (BLOCK * 10 // 17) ** -0.5, 0.375, ((0, 16), (1, 32))),
        "trace_map": bell_draw(seeds[4], (BLOCK, TRACES), BLOCK ** -0.5, 0.3125),
        "lift_map": bell_draw(seeds[5], (TRACES, BLOCK), TRACES ** -0.5, 0.3125),
        "neighbours": draw_neighbours(jax.random.fold_in(seeds[7], 71), 0),
    }


def apply_block(matrix, vector):
    return jnp.einsum('lij,lj->li', matrix.astype(jnp.float32), vector, precision=lax.Precision.HIGHEST)


def reference(right_side, inverse_blocks, lower_blocks, upper_blocks, trace_map, lift_map, neighbours):
    lines_all = right_side.shape[1]
    width = right_side.shape[2]

    def down_step(previous, pieces):
        source, inverse, lower = pieces
        value = apply_block(inverse, source - apply_block(lower, previous))
        return value, value

    start = jnp.zeros((lines_all, width), jnp.float32)
    _, forward = lax.scan(down_step, start, (right_side, inverse_blocks, lower_blocks))

    def up_step(following, pieces):
        value, inverse, upper = pieces
        result = value - apply_block(inverse, apply_block(upper, following))
        return result, result

    _, correction = lax.scan(up_step, start, (forward, inverse_blocks, upper_blocks), reverse=True)
    traces = jnp.einsum('cld,df->clf', correction, trace_map.astype(jnp.float32), precision=lax.Precision.HIGHEST)
    facevars = traces.shape[2] // 4
    pieces_list = []
    for face in range(4):
        other = face ^ 1
        across = traces[:, neighbours[:, face], other * facevars:(other + 1) * facevars]
        pieces_list.append(traces[:, :, face * facevars:(face + 1) * facevars] - across)
    jump = jnp.concatenate(pieces_list, axis=2)
    face_residual = jnp.einsum('clf,fd->cld', jump, lift_map.astype(jnp.float32), precision=lax.Precision.HIGHEST)
    return correction, face_residual
```

```python
import jax
import jax.numpy as jnp
from jax import lax
from jax.experimental import pallas as pl
from jax.experimental.pallas import tpu as pltpu
from jax.sharding import PartitionSpec as P

F32 = jnp.float32
BF16 = jnp.bfloat16
NN = (((1,), (0,)), ((), ()))
NT = (((1,), (1,)), ((), ()))
VMEM = pl.BlockSpec(memory_space=pltpu.VMEM)
SMEM = pl.BlockSpec(memory_space=pltpu.SMEM)
LIMIT = 40 * 1024 * 1024


def dot(a, b, dims=NN):
    return lax.dot_general(a, b, dims, preferred_element_type=F32)


def split(x):
    high = x.astype(BF16)
    return high, (x - high.astype(F32)).astype(BF16)


def product(a, b):
    a_high, a_low = split(a)
    b_high, b_low = split(b)
    return dot(a_high, b_high) + dot(a_high, b_low) + dot(a_low, b_high)


def stacked(row):
    high, low = split(row)
    index = lax.broadcasted_iota(jnp.int32, (16, row.shape[1]), 0)
    zero = jnp.zeros((16, row.shape[1]), F32)
    high = jnp.broadcast_to(high.astype(F32), zero.shape)
    low = jnp.broadcast_to(low.astype(F32), zero.shape)
    return jnp.where(index == 0, high, jnp.where(index == 1, low, zero)).astype(BF16)


def apply_exact(block, row):
    out = dot(stacked(row), block, NT)
    return out[0:1] + out[1:2]


def apply_pair(pair, row):
    n = pair.shape[0] // 2
    out = dot(stacked(row), pair, NT)
    return out[0:1, :n] + out[1:2, :n] + out[0:1, n:]


def apply_full(matrix, row):
    high, low = split(matrix)
    rows = stacked(row)
    main = dot(rows, high, NT)
    rest = dot(rows, low, NT)
    return main[0:1] + main[1:2] + rest[0:1]


def put_pair(ref, matrix):
    n = matrix.shape[0]
    high, low = split(matrix)
    ref[0:n] = high
    ref[n:] = low


def put_row(ref, row):
    ref[...] = jnp.broadcast_to(row, ref.shape)


def call(kernel, outs, *args, scalars=0, flops=0, name=None):
    return pl.pallas_call(
        kernel,
        out_shape=[jax.ShapeDtypeStruct(s, t) for s, t in outs],
        in_specs=[SMEM] * scalars + [VMEM] * (len(args) - scalars),
        out_specs=[VMEM] * len(outs),
        compiler_params=pltpu.CompilerParams(vmem_limit_bytes=LIMIT),
        cost_estimate=pl.CostEstimate(flops=flops, bytes_accessed=0, transcendentals=0),
        name=name,
    )(*args)


def down_kernel(core, a, l, r, give, keep):
    n = a.shape[2]

    def one(i, _):
        line = jnp.where(i == 0, 1 - core[0], core[0])
        first = dot(a[0, line], l[0, line])
        second = dot(a[1, line], l[1, line])
        total = product(second, first)
        x = apply_exact(a[0, line], r[line, 0:1])
        x = apply_exact(a[1, line], r[line, 1:2] - apply_exact(l[1, line], x))

        @pl.when(i == 0)
        def _():
            give[0:n] = total
            give[n:] = jnp.broadcast_to(x, (8, n))

        @pl.when(i == 1)
        def _():
            keep[0:n] = total
            keep[n:] = jnp.broadcast_to(x, (8, n))

        return 0

    lax.fori_loop(0, 2, one, 0)


def up_kernel(core, a, l, u, r, give_f, keep_f, give, keep):
    n = a.shape[2]

    def one(i, _):
        line = jnp.where(i == 0, 1 - core[0], core[0])
        first = dot(a[0, line], u[0, line])
        second = dot(a[1, line], u[1, line])
        back = product(first, second)
        own = dot(a[0, line], l[0, line])
        x = apply_exact(a[0, line], r[line, 0:1])

        def finish(out, f):
            out[0:n] = back
            out[n : 2 * n] = -(own + product(first, f[0:n]))
            b = x - apply_exact(a[0, line], apply_exact(u[0, line], f[n : n + 1]))
            out[2 * n :] = jnp.broadcast_to(b, (8, n))

        @pl.when(i == 0)
        def _():
            finish(give, give_f)

        @pl.when(i == 1)
        def _():
            finish(keep, keep_f)

        return 0

    lax.fori_loop(0, 2, one, 0)


def down_join_kernel(core, got, keep, total, lower, vectors):
    n = got.shape[1]

    def finish(low, high):
        put_pair(total, product(high[0:n], low[0:n]))
        put_pair(lower, low[0:n])
        a = low[n : n + 1]
        vectors[0] = jnp.broadcast_to(high[n : n + 1] + apply_full(high[0:n], a), (8, n))
        vectors[1] = jnp.broadcast_to(a, (8, n))

    @pl.when(core[0] == 0)
    def _():
        finish(keep, got)

    @pl.when(core[0] == 1)
    def _():
        finish(got, keep)


def up_join_kernel(core, got, keep, total, b_low, b_high, g_low, g_high, vectors):
    n = got.shape[1]

    def finish(low, high):
        put_pair(total, product(low[0:n], high[0:n]))
        put_pair(b_low, low[0:n])
        put_pair(b_high, high[0:n])
        put_pair(g_low, low[n : 2 * n])
        put_pair(g_high, high[n : 2 * n])
        vectors[0] = low[2 * n :]
        vectors[1] = high[2 * n :]

    @pl.when(core[0] == 0)
    def _():
        finish(keep, got)

    @pl.when(core[0] == 1)
    def _():
        finish(got, keep)


def step_kernel(came, constant, pair, out):
    put_row(out, constant[0:1] + apply_pair(pair[...], came[0:1]))


def turn_kernel(core, e, f_vectors, lower, b_vectors, b_low, g_low, g_high, b_chip, b_up, give, keep):
    enter = e[0:1]
    middle = f_vectors[1, 0:1] + apply_pair(lower[...], enter)
    up = b_vectors[1, 0:1] + apply_pair(g_high[...], middle)
    low = b_vectors[0, 0:1] + apply_pair(g_low[...], enter)
    put_row(b_chip, low + apply_pair(b_low[...], up))
    put_row(b_up, up)
    first = core[0] == 0
    put_row(give, jnp.where(first, middle, enter))
    put_row(keep, jnp.where(first, enter, middle))


def local_kernel(core, r, a, l, u, got, keep, f):
    for line in range(2):
        mine = core[0] == line
        enter = jnp.where(mine, keep[0:1], got[0:1])
        one = apply_exact(a[0, line], r[line, 0:1] - apply_exact(l[0, line], enter))
        two = apply_exact(a[1, line], r[line, 1:2] - apply_exact(l[1, line], one))
        f[line, 0:1] = one
        f[line, 1:2] = two


def middle_kernel(core, c, b_up, b_high, give, keep):
    enter = c[0:1]
    middle = b_up[0:1] + apply_pair(b_high[...], enter)
    first = core[0] == 0
    put_row(give, jnp.where(first, enter, middle))
    put_row(keep, jnp.where(first, middle, enter))


def rows_exact(block, rows):
    m = rows.shape[0]
    high, low = split(rows)
    return dot(high, block) + dot(low, block)


def last_kernel(core, got, keep, f, a, u, w, correction, traces):
    n = w.shape[0]
    parts = [[None, None], [None, None]]
    for line in range(2):
        mine = core[0] == line
        enter = jnp.where(mine, keep[0:1], got[0:1])
        two = f[line, 1:2] - apply_exact(a[1, line], apply_exact(u[1, line], enter))
        one = f[line, 0:1] - apply_exact(a[0, line], apply_exact(u[0, line], two))
        parts[0][line] = one
        parts[1][line] = two
    index = lax.broadcasted_iota(jnp.int32, (16, n), 0)
    rows = jnp.zeros((16, n), F32)
    for cell in range(2):
        for line in range(2):
            row = parts[cell][line]
            correction[cell, line : line + 1] = row
            rows = jnp.where(index == cell * 2 + line, jnp.broadcast_to(row, (16, n)), rows)
    traces[...] = rows_exact(w[...], rows)[0:8]


def jump_kernel(traces, one, other, weights, lift, residual):
    n = lift.shape[0]
    own = traces[:, 0:n]
    mine = traces[:, n:]
    index = lax.broadcasted_iota(jnp.int32, (16, n), 0)
    rows = jnp.zeros((16, n), F32)
    for cell in range(2):
        for line in range(2):
            at = cell * 2 + line
            jump = own[at : at + 1]
            for side, source in enumerate((mine, one[...], other[...])):
                for k in range(2):
                    j = cell * 2 + k
                    jump = jump - weights[line, side * 2 + k : side * 2 + k + 1] * source[j : j + 1]
            rows = jnp.where(index == at, jnp.broadcast_to(jump, (16, n)), rows)
    out = rows_exact(lift[...], rows)
    for cell in range(2):
        residual[cell] = out[cell * 2 : cell * 2 + 2]


def body(right_side, inverse_blocks, lower_blocks, upper_blocks, trace_map, lift_map, neighbours):
    n = right_side.shape[2]
    wall, tang = lax.axis_size("wall"), lax.axis_size("tang")
    chips = wall // 2
    core = lax.rem(lax.axis_index("wall"), 2)
    scalar = jnp.reshape(core, (1,))
    r = jnp.transpose(right_side, (1, 0, 2))
    across = [(i, i ^ 1) for i in range(wall)]
    row = ((8, n), F32)
    pair = ((2 * n, n), BF16)

    here = lax.axis_index("tang")
    even = lax.rem(here, 2) == 0
    after, before = lax.rem(here + 1, tang), lax.rem(here + tang - 1, tang)
    near, far = jnp.where(even, after, before), jnp.where(even, before, after)
    places = jnp.stack([2 * here, 2 * here + 1, 2 * near, 2 * near + 1, 2 * far, 2 * far + 1])
    weights = (neighbours[:, None, :] == places[None, :, None]).astype(F32)
    weights = jnp.repeat(weights, n // 4, axis=2)
    face = trace_map.reshape(n, 4, n // 4)
    swapped = jnp.stack([face[:, 1], face[:, 0], face[:, 3], face[:, 2]], axis=1).reshape(n, n)
    both = jnp.concatenate([trace_map, swapped], axis=1)

    mul = 2 * n * n * n
    give_f, keep_f = call(
        down_kernel, [((n + 8, n), F32)] * 2, scalar, inverse_blocks, lower_blocks, r,
        scalars=1, flops=10 * mul, name="down",
    )
    got_f = lax.ppermute(give_f, "wall", across)
    give_b, keep_b = call(
        up_kernel, [((2 * n + 8, n), F32)] * 2,
        scalar, inverse_blocks, lower_blocks, upper_blocks, r, give_f, keep_f,
        scalars=1, flops=18 * mul, name="up",
    )
    total, lower, f_vectors = call(
        down_join_kernel, [pair, pair, ((2, 8, n), F32)], scalar, got_f, keep_f,
        scalars=1, flops=3 * mul, name="down_join",
    )
    got_b = lax.ppermute(give_b, "wall", across)
    back, b_low, b_high, g_low, g_high, b_vectors = call(
        up_join_kernel, [pair] * 5 + [((2, 8, n), F32)], scalar, got_b, keep_b,
        scalars=1, flops=3 * mul, name="up_join",
    )

    enter = jnp.zeros((8, n), F32)
    out = f_vectors[0]
    for chip in range(chips - 1):
        came = lax.ppermute(out, "wall", [(2 * chip + c, 2 * chip + 2 + c) for c in range(2)])
        enter = enter + came
        if chip < chips - 2:
            (out,) = call(step_kernel, [row], came, f_vectors[0], total, flops=mul // 100, name="step")

    b_chip, b_up, give, keep = call(
        turn_kernel, [row] * 4,
        scalar, enter, f_vectors, lower, b_vectors, b_low, g_low, g_high,
        scalars=1, flops=mul // 50, name="turn",
    )
    got = lax.ppermute(give, "wall", across)
    (forward,) = call(
        local_kernel, [((2, 2, n), F32)],
        scalar, r, inverse_blocks, lower_blocks, upper_blocks, got, keep,
        scalars=1, flops=mul // 20, name="local",
    )

    arrive = jnp.zeros((8, n), F32)
    out = b_chip
    for chip in range(chips - 1, 0, -1):
        came = lax.ppermute(out, "wall", [(2 * chip + c, 2 * chip - 2 + c) for c in range(2)])
        arrive = arrive + came
        if chip > 1:
            (out,) = call(step_kernel, [row], came, b_chip, back, flops=mul // 100, name="step")

    give, keep = call(
        middle_kernel, [row] * 2, scalar, arrive, b_up, b_high, scalars=1, flops=mul // 100, name="middle"
    )
    got = lax.ppermute(give, "wall", across)
    correction, traces = call(
        last_kernel, [((2, 2, n), F32), ((8, 2 * n), F32)],
        scalar, got, keep, forward, inverse_blocks, upper_blocks, both,
        scalars=1, flops=mul // 20, name="last",
    )
    sent = traces[:, n:]
    first = [(i, i + 1) for i in range(0, tang, 2)]
    second = [(i, (i + 1) % tang) for i in range(1, tang, 2)]
    from_far = lax.ppermute(sent, "tang", second + [(j, i) for i, j in second])
    from_near = lax.ppermute(sent, "tang", first + [(j, i) for i, j in first])
    (residual,) = call(
        jump_kernel, [((2, 2, n), F32)], traces, from_near, from_far, weights, lift_map,
        flops=mul // 50, name="jump",
    )
    return correction, residual


def solution(mesh):
    in_specs = (
        P("wall", "tang", None),
        P("wall", "tang", None, None),
        P("wall", "tang", None, None),
        P("wall", "tang", None, None),
        P(),
        P(),
        P("tang", None),
    )
    out_specs = (P("wall", "tang", None), P("wall", "tang", None))
    return jax.shard_map(body, mesh=mesh, in_specs=in_specs, out_specs=out_specs, check_vma=False)
```

```python
import functools

import jax
import jax.numpy as jnp
from jax import lax
from jax.experimental import pallas as pl
from jax.experimental.pallas import tpu as pltpu
from jax.sharding import PartitionSpec as P

F32 = jnp.float32
BF16 = jnp.bfloat16
NN = (((1,), (0,)), ((), ()))
NT = (((1,), (1,)), ((), ()))
VMEM = pl.BlockSpec(memory_space=pltpu.VMEM)
HBM = pl.BlockSpec(memory_space=pltpu.HBM)
SMEM = pl.BlockSpec(memory_space=pltpu.SMEM)
LIMIT = 16 * 1024 * 1024
WHOLE = 48 * 1024 * 1024


def dot(a, b, dims=NN):
    return lax.dot_general(a, b, dims, preferred_element_type=F32)


def split(x):
    high = x.astype(BF16)
    return high, (x - high.astype(F32)).astype(BF16)


def product(a, b):
    a_high, a_low = split(a)
    b_high, b_low = split(b)
    return dot(a_high, b_high) + dot(a_high, b_low) + dot(a_low, b_high)


def stacked(row):
    high, low = split(row)
    index = lax.broadcasted_iota(jnp.int32, (16, row.shape[1]), 0)
    zero = jnp.zeros((16, row.shape[1]), F32)
    high = jnp.broadcast_to(high.astype(F32), zero.shape)
    low = jnp.broadcast_to(low.astype(F32), zero.shape)
    return jnp.where(index == 0, high, jnp.where(index == 1, low, zero)).astype(BF16)


def apply_exact(block, row):
    out = dot(stacked(row), block, NT)
    return out[0:1] + out[1:2]


def apply_pair(pair, row):
    n = pair.shape[0] // 2
    out = dot(stacked(row), pair, NT)
    return out[0:1, :n] + out[1:2, :n] + out[0:1, n:]


def apply_full(matrix, row):
    high, low = split(matrix)
    rows = stacked(row)
    main = dot(rows, high, NT)
    rest = dot(rows, low, NT)
    return main[0:1] + main[1:2] + rest[0:1]


def put_pair(ref, matrix):
    n = matrix.shape[0]
    high, low = split(matrix)
    ref[0:n] = high
    ref[n:] = low


def put_row(ref, row):
    ref[...] = jnp.broadcast_to(row, ref.shape)


def call(kernel, outs, *args, scalars=0, flops=0, name=None, after=()):
    count = len(args)
    operands = list(args) + list(after)

    def inner(*refs):
        kernel(*refs[:count], *refs[len(operands) :])

    return pl.pallas_call(
        inner,
        out_shape=[jax.ShapeDtypeStruct(s, t) for s, t in outs],
        in_specs=[SMEM] * scalars + [VMEM] * (len(operands) - scalars),
        out_specs=[VMEM] * len(outs),
        compiler_params=pltpu.CompilerParams(vmem_limit_bytes=LIMIT),
        cost_estimate=pl.CostEstimate(flops=flops, bytes_accessed=0, transcendentals=0),
        name=name,
    )(*operands)


def line_maps(a, l, u, r, out, ahead, back, rows):
    n = r[0].shape[1]
    a0, l0 = a(0), l(0)
    first = dot(a0, l0)
    x = apply_exact(a0, r[0])
    a1, l1 = a(1), l(1)
    up = product(dot(a1, l1), first)
    y = apply_exact(a1, r[1] - apply_exact(l1, x))
    u0 = u(0)
    near = dot(a0, u0)
    turn = -(first + product(near, up))
    x = x - apply_exact(a0, apply_exact(u0, y))
    far = dot(a1, u(1))
    down = product(near, far)
    out[0:n] = up
    out[n : 2 * n] = turn
    out[2 * n : 3 * n] = down
    index = lax.broadcasted_iota(jnp.int32, (8, n), 0)
    both = jnp.where(index == 0, jnp.broadcast_to(y, (8, n)), jnp.broadcast_to(x, (8, n)))
    out[3 * n :] = both
    rows[...] = both
    for ref, parts in ((ahead, (turn, up)), (back, (far, down))):
        for i, part in enumerate(parts):
            high, low = split(part)
            ref[i * n : (i + 1) * n] = high
            ref[(2 + i) * n : (3 + i) * n] = low


def first_kernel(line_ref, r, a, l, u, out, ahead, back, rows, r_here, a_here, l_here, u_here, sems):
    line = line_ref[0]
    copies = [pltpu.make_async_copy(r, r_here, sems.at[0])]
    for at in (line, 1 - line):
        for cell, source, here in (
            (0, a, a_here), (0, l, l_here), (1, a, a_here), (1, l, l_here), (0, u, u_here), (1, u, u_here)
        ):
            copies.append(pltpu.make_async_copy(source.at[cell, at], here.at[cell, at], sems.at[len(copies)]))
    for copy in copies:
        copy.start()

    def arrived(here, place):
        def get(cell):
            copies[place[cell]].wait()
            return here[cell, line]

        return get

    copies[0].wait()
    blocks = [arrived(a_here, (1, 3)), arrived(l_here, (2, 4)), arrived(u_here, (5, 6))]
    line_maps(*blocks, [r_here[cell, pl.ds(line, 1), :] for cell in range(2)], out, ahead, back, rows)
    for copy in copies[7:]:
        copy.wait()


def second_kernel(line_ref, r, a, l, u, out, ahead, back, rows):
    line = line_ref[0]
    blocks = [lambda cell, here=here: here[cell, line] for here in (a, l, u)]
    line_maps(*blocks, [r[cell, pl.ds(line, 1), :] for cell in range(2)], out, ahead, back, rows)


def down_join_kernel(core, got, keep, chip, total, lower, a_chip, a_low):
    n = got.shape[1]

    def finish(low, high):
        matrix = product(high[0:n], low[0:n])
        put_pair(total, matrix)
        put_pair(lower, low[0:n])
        a = low[3 * n : 3 * n + 1]
        joined = high[3 * n : 3 * n + 1] + apply_full(high[0:n], a)
        chip[0:n] = matrix
        chip[n:] = jnp.broadcast_to(joined, (8, n))
        put_row(a_chip, joined)
        put_row(a_low, a)

    @pl.when(core[0] == 0)
    def _():
        finish(keep, got)

    @pl.when(core[0] == 1)
    def _():
        finish(got, keep)


def up_join_kernel(core, got, keep, chip, total, b_low, b_high, g_low, g_high, v_low, v_high):
    n = got.shape[1]

    def finish(low, high):
        matrix = product(low[2 * n : 3 * n], high[2 * n : 3 * n])
        chip[...] = matrix
        put_pair(total, matrix)
        put_pair(b_low, low[2 * n : 3 * n])
        put_pair(b_high, high[2 * n : 3 * n])
        put_pair(g_low, low[n : 2 * n])
        put_pair(g_high, high[n : 2 * n])
        put_row(v_low, low[3 * n + 1 : 3 * n + 2])
        put_row(v_high, high[3 * n + 1 : 3 * n + 2])

    @pl.when(core[0] == 0)
    def _():
        finish(keep, got)

    @pl.when(core[0] == 1)
    def _():
        finish(got, keep)


def pair_row_kernel(came, pair, row):
    n = came.shape[1]
    put_pair(pair, came[0:n])
    row[...] = came[n:]


def pair_kernel(came, pair, token):
    put_pair(pair, came[...])
    token[...] = jnp.zeros(token.shape, F32)


def total_of(refs):
    out = refs[0][0:1]
    for ref in refs[1:]:
        out = out + ref[0:1]
    return out


def step_kernel(constant, pair, *refs):
    *x, out = refs
    put_row(out, constant[0:1] + apply_pair(pair[...], total_of(x)))


def entering(before, y, x):
    return total_of(x) + apply_pair(before[...], total_of(y))


def jump_step_kernel(many, before, constant, pair, *refs):
    *x, out = refs
    put_row(out, constant[0:1] + apply_pair(pair[...], entering(before, x[:many], x[many:])))


def turn_kernel(many, before, a_low, lower, v_low, v_high, b_low, g_low, g_high, *refs):
    *x, b_chip = refs
    enter = entering(before, x[:many], x[many:])
    middle = a_low[0:1] + apply_pair(lower[...], enter)
    up = v_high[0:1] + apply_pair(g_high[...], middle)
    low = v_low[0:1] + apply_pair(g_low[...], enter)
    put_row(b_chip, low + apply_pair(b_low[...], up))


def spread_kernel(many, core, before, a_low, lower, v_high, g_high, *refs):
    *x, b_up, give, keep = refs
    enter = entering(before, x[:many], x[many:])
    middle = a_low[0:1] + apply_pair(lower[...], enter)
    put_row(b_up, v_high[0:1] + apply_pair(g_high[...], middle))
    first = core[0] == 0
    put_row(give, jnp.where(first, middle, enter))
    put_row(keep, jnp.where(first, enter, middle))


def local_kernel(size, core, here, near, give_map, keep_map, give_rows, keep_rows, got, keep, f, weights):
    n = got.shape[1]
    column = lax.broadcasted_iota(jnp.int32, (1, n), 1)
    at = here[0]
    up, down = lax.rem(at + 1, size), lax.rem(at + size - 1, size)
    even = lax.rem(at, 2) == 0
    sides = (at, jnp.where(even, up, down), jnp.where(even, down, up))
    places = [2 * side + k for side in sides for k in range(2)]
    for i, (maps, rows, enter) in enumerate(((give_map, give_rows, got), (keep_map, keep_rows, keep))):
        moved = apply_pair(maps[...], enter[0:1])
        f[i, 0:1] = rows[1:2] + moved[:, :n]
        f[i, 1:2] = rows[0:1] + moved[:, n:]
    for line in range(2):
        for k in range(6):
            row = jnp.zeros((1, n), F32)
            for face in range(4):
                inside = (column >= face * (n // 4)) & (column < (face + 1) * (n // 4))
                meets = near[line, face] == places[k]
                row = jnp.where(inside, jnp.where(meets, 1.0, 0.0), row)
            weights[line, k : k + 1] = row


def middle_kernel(many, core, before, b_up, b_high, *refs):
    *x, give, keep = refs
    enter = entering(before, x[:many], x[many:])
    middle = b_up[0:1] + apply_pair(b_high[...], enter)
    first = core[0] == 0
    put_row(give, jnp.where(first, enter, middle))
    put_row(keep, jnp.where(first, middle, enter))


def rows_exact(block, rows):
    high, low = split(rows)
    return dot(high, block) + dot(low, block)


def last_kernel(core, got, keep, f, give_map, keep_map, w, correction, own, sent):
    n = w.shape[0]
    values = []
    for i, (maps, enter) in enumerate(((give_map, got), (keep_map, keep))):
        moved = apply_pair(maps[...], enter[0:1])
        values.append((f[i, 0:1] + moved[:, n:], f[i, 1:2] - moved[:, :n]))
    index = lax.broadcasted_iota(jnp.int32, (16, n), 0)
    rows = jnp.zeros((16, n), F32)
    first = core[0] == 0
    for cell in range(2):
        given, own_row = values[0][cell], values[1][cell]
        for line, row in enumerate((jnp.where(first, own_row, given), jnp.where(first, given, own_row))):
            correction[cell, line : line + 1] = row
            rows = jnp.where(index == cell * 2 + line, jnp.broadcast_to(row, (16, n)), rows)
    traces = rows_exact(w[...], rows)[0:8]
    own[...] = traces
    width = n // 4
    column = lax.broadcasted_iota(jnp.int32, (8, n), 1)
    lower = (column < width) | ((column >= 2 * width) & (column < 3 * width))
    sent[...] = jnp.where(lower, pltpu.roll(traces, n - width, 1), pltpu.roll(traces, width, 1))


def jump_kernel(own, mine, one, other, weights, lift, residual):
    n = lift.shape[0]
    index = lax.broadcasted_iota(jnp.int32, (16, n), 0)
    rows = jnp.zeros((16, n), F32)
    for cell in range(2):
        for line in range(2):
            at = cell * 2 + line
            jump = own[at : at + 1]
            for side, source in enumerate((mine, one, other)):
                for k in range(2):
                    j = cell * 2 + k
                    jump = jump - weights[line, side * 2 + k : side * 2 + k + 1] * source[j : j + 1]
            rows = jnp.where(index == at, jnp.broadcast_to(jump, (16, n)), rows)
    out = rows_exact(lift[...], rows)
    for cell in range(2):
        residual[cell] = out[cell * 2 : cell * 2 + 2]


def chips_to(pairs):
    return [(2 * i + c, 2 * j + c) for i, j in pairs for c in range(2)]


def body(right_side, inverse_blocks, lower_blocks, upper_blocks, trace_map, lift_map, neighbours):
    n = right_side.shape[2]
    wall, tang = lax.axis_size("wall"), lax.axis_size("tang")
    chips = wall // 2
    jumps = chips // 4
    singles = chips - 2 * jumps
    core = lax.rem(lax.axis_index("wall"), 2)
    own_line = jnp.reshape(core, (1,))
    other_line = 1 - own_line
    r, a, l, u = right_side, inverse_blocks, lower_blocks, upper_blocks
    across = [(i, i ^ 1) for i in range(wall)]
    row = ((8, n), F32)
    pair = ((2 * n, n), BF16)
    joined = ((n + 8, n), F32)

    here = jnp.reshape(lax.axis_index("tang"), (1,))

    mul = 2 * n * n * n
    maps = [((3 * n + 8, n), F32), ((4 * n, n), BF16), ((4 * n, n), BF16), row]
    here_now = [(r.shape, F32)] + [(a.shape, BF16)] * 3
    give, give_ahead, give_back, give_rows, r, a, l, u = pl.pallas_call(
        first_kernel,
        out_shape=[jax.ShapeDtypeStruct(*x) for x in maps + here_now],
        in_specs=[SMEM] + [HBM] * 4,
        out_specs=[VMEM] * 8,
        scratch_shapes=[pltpu.SemaphoreType.DMA((13,))],
        compiler_params=pltpu.CompilerParams(vmem_limit_bytes=WHOLE),
        cost_estimate=pl.CostEstimate(flops=13 * mul, bytes_accessed=0, transcendentals=0),
        name="first",
    )(other_line, r, a, l, u)
    got = lax.ppermute(give, "wall", across)
    keep, keep_ahead, keep_back, keep_rows = call(
        second_kernel, maps, own_line, r, a, l, u, scalars=1, flops=13 * mul, name="second"
    )
    chip_f, total, lower, a_chip, a_low = call(
        down_join_kernel, [joined, pair, pair, row, row], own_line, got, keep,
        scalars=1, flops=3 * mul, name="down_join",
    )
    chip_b, back, b_low, b_high, g_low, g_high, v_low, v_high = call(
        up_join_kernel, [((n, n), F32)] + [pair] * 5 + [row] * 2, own_line, got, keep,
        scalars=1, flops=3 * mul, name="up_join", after=(a_chip,),
    )
    moved_b = lax.ppermute(chip_b, "wall", chips_to([(k, k - 1) for k in range(chips - 2, 0, -2)]))

    moved_f = lax.ppermute(
        chip_f, "wall", chips_to([(k, k + 1) for k in range(singles, chips, 2)])
    )
    x, y = [], []
    out = a_chip
    for k in range(1, singles):
        x.append(lax.ppermute(out, "wall", chips_to([(k - 1, k)])))
        (out,) = call(step_kernel, [row], a_chip, total, *x, flops=mul // 100, name="step")
    pre, pre_row = call(pair_row_kernel, [pair, row], moved_f, flops=mul // 10, name="pre")
    for k in range(jumps):
        last = singles + 2 * k - 1
        y.append(lax.ppermute(out, "wall", chips_to([(last, last + 2)])))
        if k == jumps - 1:
            side = lax.ppermute(
                out, "wall", chips_to([(singles + 2 * j - 1, singles + 2 * j) for j in range(jumps)])
            )
        else:
            (out,) = call(
                functools.partial(jump_step_kernel, k + 1), [row], pre, a_chip, total, *y, *x, pre_row,
                flops=mul // 50, name="jump_step",
            )
    x = [*x, side, pre_row]
    entry, token = call(pair_kernel, [pair, row], moved_b, flops=mul // 10, name="entry")
    (b_chip,) = call(
        functools.partial(turn_kernel, jumps), [row],
        pre, a_low, lower, v_low, v_high, b_low, g_low, g_high, *y, *x,
        flops=mul // 50, name="turn", after=(token,),
    )

    odd = list(range(chips - 1, 0, -2))
    z = []
    out = b_chip
    waits = ()
    for k in odd[1:]:
        z.append(lax.ppermute(out, "wall", chips_to([(k + 2, k)])))
        if len(z) == 1:
            sent = lax.ppermute(b_chip, "wall", chips_to([(j, j - 1) for j in range(chips - 2, 0, -2)]))
        if k == 1:
            done = out
            b_up, give, keep = call(
                functools.partial(spread_kernel, jumps), [row] * 3, own_line, pre, a_low, lower, v_high, g_high, *y, *x,
                scalars=1, flops=mul // 50, name="spread",
            )
            got = lax.ppermute(give, "wall", across)
            forward, weights = call(
                functools.partial(local_kernel, tang), [((2, 2, n), F32), ((2, 8, n), F32)],
            own_line, here, neighbours, give_ahead, keep_ahead, give_rows, keep_rows, got, keep,
                scalars=3, flops=mul // 20, name="local",
            )
            waits = (weights,)
        (out,) = call(
            functools.partial(jump_step_kernel, len(z)), [row], entry, b_chip, back, *z, sent,
            flops=mul // 50, name="back_step", after=waits,
        )
    ends = lax.ppermute(out, "wall", chips_to([(k, k - 1) for k in odd]))

    give, keep = call(
        functools.partial(middle_kernel, len(z)), [row] * 2, own_line, entry, b_up, b_high, *z, sent, ends,
        scalars=1, flops=mul // 100, name="middle", after=(forward,),
    )
    got = lax.ppermute(give, "wall", across)
    correction, traces, sent = call(
        last_kernel, [((2, 2, n), F32), row, row], own_line, got, keep, forward, give_back, keep_back, trace_map,
        scalars=1, flops=mul // 20, name="last",
    )
    first = [(i, i + 1) for i in range(0, tang, 2)]
    second = [(i, (i + 1) % tang) for i in range(1, tang, 2)]
    from_near = lax.ppermute(sent, "tang", first + [(j, i) for i, j in first])
    from_far = lax.ppermute(sent, "tang", second + [(j, i) for i, j in second])
    (residual,) = call(
        jump_kernel, [((2, 2, n), F32)], traces, sent, from_near, from_far, weights, lift_map,
        flops=mul // 50, name="jump",
    )
    return correction, residual


def solution(mesh):
    in_specs = (
        P("wall", "tang", None),
        P("wall", "tang", None, None),
        P("wall", "tang", None, None),
        P("wall", "tang", None, None),
        P(),
        P(),
        P("tang", None),
    )
    out_specs = (P("wall", "tang", None), P("wall", "tang", None))
    return jax.shard_map(body, mesh=mesh, in_specs=in_specs, out_specs=out_specs, check_vma=False)
```

```python
import functools

import jax
import jax.numpy as jnp
from jax import lax
from jax.experimental import pallas as pl
from jax.experimental.pallas import tpu as pltpu
from jax.sharding import PartitionSpec as P

F32 = jnp.float32
BF16 = jnp.bfloat16
NN = (((1,), (0,)), ((), ()))
NT = (((1,), (1,)), ((), ()))
VMEM = pl.BlockSpec(memory_space=pltpu.VMEM)
HBM = pl.BlockSpec(memory_space=pltpu.HBM)
SMEM = pl.BlockSpec(memory_space=pltpu.SMEM)
LIMIT = 16 * 1024 * 1024
WHOLE = 48 * 1024 * 1024


def dot(a, b, dims=NN):
    return lax.dot_general(a, b, dims, preferred_element_type=F32)


def split(x):
    high = x.astype(BF16)
    return high, (x - high.astype(F32)).astype(BF16)


def product(a, b):
    a_high, a_low = split(a)
    b_high, b_low = split(b)
    return dot(a_high, b_high) + dot(a_high, b_low) + dot(a_low, b_high)


def stacked(row):
    high, low = split(row)
    index = lax.broadcasted_iota(jnp.int32, (16, row.shape[1]), 0)
    zero = jnp.zeros((16, row.shape[1]), F32)
    high = jnp.broadcast_to(high.astype(F32), zero.shape)
    low = jnp.broadcast_to(low.astype(F32), zero.shape)
    return jnp.where(index == 0, high, jnp.where(index == 1, low, zero)).astype(BF16)


def apply_exact(block, row):
    out = dot(stacked(row), block, NT)
    return out[0:1] + out[1:2]


def apply_pair(pair, row):
    n = pair.shape[0] // 2
    out = dot(stacked(row), pair, NT)
    return out[0:1, :n] + out[1:2, :n] + out[0:1, n:]


def apply_full(matrix, row):
    high, low = split(matrix)
    rows = stacked(row)
    main = dot(rows, high, NT)
    rest = dot(rows, low, NT)
    return main[0:1] + main[1:2] + rest[0:1]


def put_pair(ref, matrix):
    n = matrix.shape[0]
    high, low = split(matrix)
    ref[0:n] = high
    ref[n:] = low


def put_row(ref, row):
    ref[...] = jnp.broadcast_to(row, ref.shape)


def call(kernel, outs, *args, scalars=0, flops=0, name=None, after=()):
    count = len(args)
    operands = list(args) + list(after)

    def inner(*refs):
        kernel(*refs[:count], *refs[len(operands) :])

    return pl.pallas_call(
        inner,
        out_shape=[jax.ShapeDtypeStruct(s, t) for s, t in outs],
        in_specs=[SMEM] * scalars + [VMEM] * (len(operands) - scalars),
        out_specs=[VMEM] * len(outs),
        compiler_params=pltpu.CompilerParams(vmem_limit_bytes=LIMIT),
        cost_estimate=pl.CostEstimate(flops=flops, bytes_accessed=0, transcendentals=0),
        name=name,
    )(*operands)


def line_maps(a, l, u, r, out, ahead, back, rows):
    n = r[0].shape[1]
    a0, l0 = a(0), l(0)
    first = dot(a0, l0)
    x = apply_exact(a0, r[0])
    a1, l1 = a(1), l(1)
    up = product(dot(a1, l1), first)
    y = apply_exact(a1, r[1] - apply_exact(l1, x))
    u0 = u(0)
    near = dot(a0, u0)
    turn = -(first + product(near, up))
    x = x - apply_exact(a0, apply_exact(u0, y))
    far = dot(a1, u(1))
    down = product(near, far)
    out[0:n] = up
    out[n : 2 * n] = turn
    out[2 * n : 3 * n] = down
    index = lax.broadcasted_iota(jnp.int32, (8, n), 0)
    both = jnp.where(index == 0, jnp.broadcast_to(y, (8, n)), jnp.broadcast_to(x, (8, n)))
    out[3 * n :] = both
    rows[...] = both
    for ref, parts in ((ahead, (turn, up)), (back, (far, down))):
        for i, part in enumerate(parts):
            high, low = split(part)
            ref[i * n : (i + 1) * n] = high
            ref[(2 + i) * n : (3 + i) * n] = low


def first_kernel(line_ref, r, a, l, u, out, ahead, back, rows, r_here, a_here, l_here, u_here, sems):
    line = line_ref[0]
    copies = [pltpu.make_async_copy(r, r_here, sems.at[0])]
    for at in (line, 1 - line):
        for cell, source, here in (
            (0, a, a_here), (0, l, l_here), (1, a, a_here), (1, l, l_here), (0, u, u_here), (1, u, u_here)
        ):
            copies.append(pltpu.make_async_copy(source.at[cell, at], here.at[cell, at], sems.at[len(copies)]))
    for copy in copies:
        copy.start()

    def arrived(here, place):
        def get(cell):
            copies[place[cell]].wait()
            return here[cell, line]

        return get

    copies[0].wait()
    blocks = [arrived(a_here, (1, 3)), arrived(l_here, (2, 4)), arrived(u_here, (5, 6))]
    line_maps(*blocks, [r_here[cell, pl.ds(line, 1), :] for cell in range(2)], out, ahead, back, rows)
    for copy in copies[7:]:
        copy.wait()


def second_kernel(line_ref, r, a, l, u, out, ahead, back, rows):
    line = line_ref[0]
    blocks = [lambda cell, here=here: here[cell, line] for here in (a, l, u)]
    line_maps(*blocks, [r[cell, pl.ds(line, 1), :] for cell in range(2)], out, ahead, back, rows)


def down_join_kernel(core, got, keep, chip, total, lower, a_chip, a_low):
    n = got.shape[1]

    def finish(low, high):
        matrix = product(high[0:n], low[0:n])
        put_pair(total, matrix)
        put_pair(lower, low[0:n])
        a = low[3 * n : 3 * n + 1]
        joined = high[3 * n : 3 * n + 1] + apply_full(high[0:n], a)
        chip[0:n] = matrix
        chip[n:] = jnp.broadcast_to(joined, (8, n))
        put_row(a_chip, joined)
        put_row(a_low, a)

    @pl.when(core[0] == 0)
    def _():
        finish(keep, got)

    @pl.when(core[0] == 1)
    def _():
        finish(got, keep)


def up_join_kernel(core, got, keep, chip, total, b_low, b_high, g_low, g_high, v_low, v_high):
    n = got.shape[1]

    def finish(low, high):
        matrix = product(low[2 * n : 3 * n], high[2 * n : 3 * n])
        chip[...] = matrix
        put_pair(total, matrix)
        put_pair(b_low, low[2 * n : 3 * n])
        put_pair(b_high, high[2 * n : 3 * n])
        put_pair(g_low, low[n : 2 * n])
        put_pair(g_high, high[n : 2 * n])
        put_row(v_low, low[3 * n + 1 : 3 * n + 2])
        put_row(v_high, high[3 * n + 1 : 3 * n + 2])

    @pl.when(core[0] == 0)
    def _():
        finish(keep, got)

    @pl.when(core[0] == 1)
    def _():
        finish(got, keep)


def pair_row_kernel(came, pair, row):
    n = came.shape[1]
    put_pair(pair, came[0:n])
    row[...] = came[n:]


def pair_kernel(came, pair, token):
    put_pair(pair, came[...])
    token[...] = jnp.zeros(token.shape, F32)


def total_of(refs):
    out = refs[0][0:1]
    for ref in refs[1:]:
        out = out + ref[0:1]
    return out


def step_kernel(constant, pair, *refs):
    *x, out = refs
    put_row(out, constant[0:1] + apply_pair(pair[...], total_of(x)))


def entering(before, y, x):
    return total_of(x) + apply_pair(before[...], total_of(y))


def jump_step_kernel(many, before, constant, pair, *refs):
    *x, out = refs
    put_row(out, constant[0:1] + apply_pair(pair[...], entering(before, x[:many], x[many:])))


def turn_kernel(many, before, a_low, lower, v_low, v_high, b_low, g_low, g_high, *refs):
    *x, b_chip = refs
    enter = entering(before, x[:many], x[many:])
    middle = a_low[0:1] + apply_pair(lower[...], enter)
    up = v_high[0:1] + apply_pair(g_high[...], middle)
    low = v_low[0:1] + apply_pair(g_low[...], enter)
    put_row(b_chip, low + apply_pair(b_low[...], up))


def spread_kernel(many, core, before, a_low, lower, v_high, g_high, *refs):
    *x, b_up, give, keep = refs
    enter = entering(before, x[:many], x[many:])
    middle = a_low[0:1] + apply_pair(lower[...], enter)
    put_row(b_up, v_high[0:1] + apply_pair(g_high[...], middle))
    first = core[0] == 0
    put_row(give, jnp.where(first, middle, enter))
    put_row(keep, jnp.where(first, enter, middle))


def local_kernel(size, core, here, near, give_map, keep_map, give_rows, keep_rows, got, keep, f, weights):
    n = got.shape[1]
    column = lax.broadcasted_iota(jnp.int32, (1, n), 1)
    at = here[0]
    up, down = lax.rem(at + 1, size), lax.rem(at + size - 1, size)
    even = lax.rem(at, 2) == 0
    sides = (at, jnp.where(even, up, down), jnp.where(even, down, up))
    places = [2 * side + k for side in sides for k in range(2)]
    for i, (maps, rows, enter) in enumerate(((give_map, give_rows, got), (keep_map, keep_rows, keep))):
        moved = apply_pair(maps[...], enter[0:1])
        f[i, 0:1] = rows[1:2] + moved[:, :n]
        f[i, 1:2] = rows[0:1] + moved[:, n:]
    for line in range(2):
        for k in range(6):
            row = jnp.zeros((1, n), F32)
            for face in range(4):
                inside = (column >= face * (n // 4)) & (column < (face + 1) * (n // 4))
                meets = near[line, face] == places[k]
                row = jnp.where(inside, jnp.where(meets, 1.0, 0.0), row)
            weights[line, k : k + 1] = row


def middle_kernel(many, core, before, b_up, b_high, *refs):
    *x, give, keep = refs
    enter = entering(before, x[:many], x[many:])
    middle = b_up[0:1] + apply_pair(b_high[...], enter)
    first = core[0] == 0
    put_row(give, jnp.where(first, enter, middle))
    put_row(keep, jnp.where(first, middle, enter))


def rows_exact(block, rows):
    high, low = split(rows)
    return dot(high, block) + dot(low, block)


def last_kernel(core, got, keep, f, give_map, keep_map, w, correction, own, sent):
    n = w.shape[0]
    values = []
    for i, (maps, enter) in enumerate(((give_map, got), (keep_map, keep))):
        moved = apply_pair(maps[...], enter[0:1])
        values.append((f[i, 0:1] + moved[:, n:], f[i, 1:2] - moved[:, :n]))
    index = lax.broadcasted_iota(jnp.int32, (16, n), 0)
    rows = jnp.zeros((16, n), F32)
    first = core[0] == 0
    for cell in range(2):
        given, own_row = values[0][cell], values[1][cell]
        for line, row in enumerate((jnp.where(first, own_row, given), jnp.where(first, given, own_row))):
            correction[cell, line : line + 1] = row
            rows = jnp.where(index == cell * 2 + line, jnp.broadcast_to(row, (16, n)), rows)
    traces = rows_exact(w[...], rows)[0:8]
    own[...] = traces
    width = n // 4
    column = lax.broadcasted_iota(jnp.int32, (8, n), 1)
    lower = (column < width) | ((column >= 2 * width) & (column < 3 * width))
    sent[...] = jnp.where(lower, pltpu.roll(traces, n - width, 1), pltpu.roll(traces, width, 1))


def jump_kernel(own, mine, one, other, weights, lift, residual):
    n = lift.shape[0]
    index = lax.broadcasted_iota(jnp.int32, (16, n), 0)
    rows = jnp.zeros((16, n), F32)
    for cell in range(2):
        for line in range(2):
            at = cell * 2 + line
            jump = own[at : at + 1]
            for side, source in enumerate((mine, one, other)):
                for k in range(2):
                    j = cell * 2 + k
                    jump = jump - weights[line, side * 2 + k : side * 2 + k + 1] * source[j : j + 1]
            rows = jnp.where(index == at, jnp.broadcast_to(jump, (16, n)), rows)
    out = rows_exact(lift[...], rows)
    for cell in range(2):
        residual[cell] = out[cell * 2 : cell * 2 + 2]


def chips_to(pairs):
    return [(2 * i + c, 2 * j + c) for i, j in pairs for c in range(2)]


def body(right_side, inverse_blocks, lower_blocks, upper_blocks, trace_map, lift_map, neighbours):
    n = right_side.shape[2]
    wall, tang = lax.axis_size("wall"), lax.axis_size("tang")
    chips = wall // 2
    jumps = chips // 4
    singles = chips - 2 * jumps
    core = lax.rem(lax.axis_index("wall"), 2)
    own_line = jnp.reshape(core, (1,))
    other_line = 1 - own_line
    r, a, l, u = right_side, inverse_blocks, lower_blocks, upper_blocks
    across = [(i, i ^ 1) for i in range(wall)]
    row = ((8, n), F32)
    pair = ((2 * n, n), BF16)
    joined = ((n + 8, n), F32)

    here = jnp.reshape(lax.axis_index("tang"), (1,))

    mul = 2 * n * n * n
    maps = [((3 * n + 8, n), F32), ((4 * n, n), BF16), ((4 * n, n), BF16), row]
    here_now = [(r.shape, F32)] + [(a.shape, BF16)] * 3
    give, give_ahead, give_back, give_rows, r, a, l, u = pl.pallas_call(
        first_kernel,
        out_shape=[jax.ShapeDtypeStruct(*x) for x in maps + here_now],
        in_specs=[SMEM] + [HBM] * 4,
        out_specs=[VMEM] * 8,
        scratch_shapes=[pltpu.SemaphoreType.DMA((13,))],
        compiler_params=pltpu.CompilerParams(vmem_limit_bytes=WHOLE),
        cost_estimate=pl.CostEstimate(flops=13 * mul, bytes_accessed=0, transcendentals=0),
        name="first",
    )(other_line, r, a, l, u)
    got = lax.ppermute(give, "wall", across)
    keep, keep_ahead, keep_back, keep_rows = call(
        second_kernel, maps, own_line, r, a, l, u, scalars=1, flops=13 * mul, name="second"
    )
    chip_f, total, lower, a_chip, a_low = call(
        down_join_kernel, [joined, pair, pair, row, row], own_line, got, keep,
        scalars=1, flops=3 * mul, name="down_join",
    )
    chip_b, back, b_low, b_high, g_low, g_high, v_low, v_high = call(
        up_join_kernel, [((n, n), F32)] + [pair] * 5 + [row] * 2, own_line, got, keep,
        scalars=1, flops=3 * mul, name="up_join", after=(a_chip,),
    )
    moved_b = lax.ppermute(chip_b, "wall", chips_to([(k, k - 1) for k in range(chips - 2, 0, -2)]))

    moved_f = lax.ppermute(
        chip_f, "wall", chips_to([(k, k + 1) for k in range(singles, chips, 2)])
    )
    x, y = [], []
    out = a_chip
    for k in range(1, singles):
        x.append(lax.ppermute(out, "wall", chips_to([(k - 1, k)])))
        (out,) = call(step_kernel, [row], a_chip, total, *x, flops=mul // 100, name="step")
    pre, pre_row = call(pair_row_kernel, [pair, row], moved_f, flops=mul // 10, name="pre")
    for k in range(jumps):
        last = singles + 2 * k - 1
        y.append(lax.ppermute(out, "wall", chips_to([(last, last + 2)])))
        if k == jumps - 1:
            side = lax.ppermute(
                out, "wall", chips_to([(singles + 2 * j - 1, singles + 2 * j) for j in range(jumps)])
            )
        else:
            (out,) = call(
                functools.partial(jump_step_kernel, k + 1), [row], pre, a_chip, total, *y, *x, pre_row,
                flops=mul // 50, name="jump_step",
            )
    x = [*x, side, pre_row]
    entry, token = call(pair_kernel, [pair, row], moved_b, flops=mul // 10, name="entry")
    (b_chip,) = call(
        functools.partial(turn_kernel, jumps), [row],
        pre, a_low, lower, v_low, v_high, b_low, g_low, g_high, *y, *x,
        flops=mul // 50, name="turn", after=(token,),
    )

    odd = list(range(chips - 1, 0, -2))
    z = []
    out = b_chip
    waits = ()
    for k in odd[1:]:
        z.append(lax.ppermute(out, "wall", chips_to([(k + 2, k)])))
        if len(z) == 1:
            sent = lax.ppermute(b_chip, "wall", chips_to([(j, j - 1) for j in range(chips - 2, 0, -2)]))
        if k == 1:
            done = out
            upper_ends = lax.ppermute(out, "wall", chips_to([(j, j - 1) for j in odd[:-1]]))
            b_up, give, keep = call(
                functools.partial(spread_kernel, jumps), [row] * 3, own_line, pre, a_low, lower, v_high, g_high, *y, *x,
                scalars=1, flops=mul // 50, name="spread",
            )
            got = lax.ppermute(give, "wall", across)
            forward, weights = call(
                functools.partial(local_kernel, tang), [((2, 2, n), F32), ((2, 8, n), F32)],
            own_line, here, neighbours, give_ahead, keep_ahead, give_rows, keep_rows, got, keep,
                scalars=3, flops=mul // 20, name="local",
            )
            waits = (weights,)
        (out,) = call(
            functools.partial(jump_step_kernel, len(z)), [row], entry, b_chip, back, *z, sent,
            flops=mul // 50, name="back_step", after=waits,
        )
    ends = lax.ppermute(out, "wall", chips_to([(1, 0)]))

    give, keep = call(
        functools.partial(middle_kernel, len(z)), [row] * 2, own_line, entry, b_up, b_high, *z, sent, ends, upper_ends,
        scalars=1, flops=mul // 100, name="middle", after=(forward,),
    )
    got = lax.ppermute(give, "wall", across)
    correction, traces, sent = call(
        last_kernel, [((2, 2, n), F32), row, row], own_line, got, keep, forward, give_back, keep_back, trace_map,
        scalars=1, flops=mul // 20, name="last",
    )
    first = [(i, i + 1) for i in range(0, tang, 2)]
    second = [(i, (i + 1) % tang) for i in range(1, tang, 2)]
    from_near = lax.ppermute(sent, "tang", first + [(j, i) for i, j in first])
    from_far = lax.ppermute(sent, "tang", second + [(j, i) for i, j in second])
    (residual,) = call(
        jump_kernel, [((2, 2, n), F32)], traces, sent, from_near, from_far, weights, lift_map,
        flops=mul // 50, name="jump",
    )
    return correction, residual


def solution(mesh):
    in_specs = (
        P("wall", "tang", None),
        P("wall", "tang", None, None),
        P("wall", "tang", None, None),
        P("wall", "tang", None, None),
        P(),
        P(),
        P("tang", None),
    )
    out_specs = (P("wall", "tang", None), P("wall", "tang", None))
    return jax.shard_map(body, mesh=mesh, in_specs=in_specs, out_specs=out_specs, check_vma=False)
```

```python
import functools

import jax
import jax.numpy as jnp
from jax import lax
from jax.experimental import pallas as pl
from jax.experimental.pallas import tpu as pltpu
from jax.sharding import PartitionSpec as P

F32 = jnp.float32
BF16 = jnp.bfloat16
NN = (((1,), (0,)), ((), ()))
NT = (((1,), (1,)), ((), ()))
VMEM = pl.BlockSpec(memory_space=pltpu.VMEM)
HBM = pl.BlockSpec(memory_space=pltpu.HBM)
SMEM = pl.BlockSpec(memory_space=pltpu.SMEM)
LIMIT = 16 * 1024 * 1024
WHOLE = 48 * 1024 * 1024


def dot(a, b, dims=NN):
    return lax.dot_general(a, b, dims, preferred_element_type=F32)


def split(x):
    high = x.astype(BF16)
    return high, (x - high.astype(F32)).astype(BF16)


def product(a, b):
    a_high, a_low = split(a)
    b_high, b_low = split(b)
    return dot(a_high, b_high) + dot(a_high, b_low) + dot(a_low, b_high)


def stacked(row):
    high, low = split(row)
    index = lax.broadcasted_iota(jnp.int32, (16, row.shape[1]), 0)
    zero = jnp.zeros((16, row.shape[1]), F32)
    high = jnp.broadcast_to(high.astype(F32), zero.shape)
    low = jnp.broadcast_to(low.astype(F32), zero.shape)
    return jnp.where(index == 0, high, jnp.where(index == 1, low, zero)).astype(BF16)


def apply_exact(block, row):
    out = dot(stacked(row), block, NT)
    return out[0:1] + out[1:2]


def apply_pair(pair, row):
    n = pair.shape[0] // 2
    out = dot(stacked(row), pair, NT)
    return out[0:1, :n] + out[1:2, :n] + out[0:1, n:]


def apply_full(matrix, row):
    high, low = split(matrix)
    rows = stacked(row)
    main = dot(rows, high, NT)
    rest = dot(rows, low, NT)
    return main[0:1] + main[1:2] + rest[0:1]


def put_pair(ref, matrix):
    n = matrix.shape[0]
    high, low = split(matrix)
    ref[0:n] = high
    ref[n:] = low


def put_row(ref, row):
    ref[...] = jnp.broadcast_to(row, ref.shape)


def call(kernel, outs, *args, scalars=0, flops=0, name=None, after=()):
    count = len(args)
    operands = list(args) + list(after)

    def inner(*refs):
        kernel(*refs[:count], *refs[len(operands) :])

    return pl.pallas_call(
        inner,
        out_shape=[jax.ShapeDtypeStruct(s, t) for s, t in outs],
        in_specs=[SMEM] * scalars + [VMEM] * (len(operands) - scalars),
        out_specs=[VMEM] * len(outs),
        compiler_params=pltpu.CompilerParams(vmem_limit_bytes=LIMIT),
        cost_estimate=pl.CostEstimate(flops=flops, bytes_accessed=0, transcendentals=0),
        name=name,
    )(*operands)


def line_maps(a, l, u, r, out, ahead, back, rows, sent=lambda part: None):
    n = r[0].shape[1]
    a0, l0 = a(0), l(0)
    first = dot(a0, l0)
    x = apply_exact(a0, r[0])
    a1, l1 = a(1), l(1)
    up = product(dot(a1, l1), first)
    out[0:n] = up
    sent(0)
    y = apply_exact(a1, r[1] - apply_exact(l1, x))
    u0 = u(0)
    near = dot(a0, u0)
    turn = -(first + product(near, up))
    out[n : 2 * n] = turn
    sent(1)
    x = x - apply_exact(a0, apply_exact(u0, y))
    far = dot(a1, u(1))
    down = product(near, far)
    out[2 * n : 3 * n] = down
    index = lax.broadcasted_iota(jnp.int32, (8, n), 0)
    both = jnp.where(index == 0, jnp.broadcast_to(y, (8, n)), jnp.broadcast_to(x, (8, n)))
    out[3 * n :] = both
    sent(2)
    rows[...] = both
    for ref, parts in ((ahead, (turn, up)), (back, (far, down))):
        for i, part in enumerate(parts):
            high, low = split(part)
            ref[i * n : (i + 1) * n] = high
            ref[(2 + i) * n : (3 + i) * n] = low


def first_kernel(line_ref, r, a, l, u, given, ahead, back, rows, r_here, a_here, l_here, u_here, out, sems, out_sems):
    line = line_ref[0]
    copies = [pltpu.make_async_copy(r, r_here, sems.at[0])]
    for at in (line, 1 - line):
        for cell, source, here in (
            (0, a, a_here), (0, l, l_here), (1, a, a_here), (1, l, l_here), (0, u, u_here), (1, u, u_here)
        ):
            copies.append(pltpu.make_async_copy(source.at[cell, at], here.at[cell, at], sems.at[len(copies)]))
    for copy in copies[:7]:
        copy.start()

    def arrived(here, place):
        def get(cell):
            copies[place[cell]].wait()
            if place[cell] == 5:
                for copy in copies[7:]:
                    copy.start()
            return here[cell, line]

        return get

    n = r.shape[2]
    parts = []
    for i, (start, size) in enumerate(((0, n), (n, n), (2 * n, n + 8))):
        at = pl.ds(start, size)
        parts.append(pltpu.make_async_copy(out.at[at], given.at[at], out_sems.at[i]))

    copies[0].wait()
    blocks = [arrived(a_here, (1, 3)), arrived(l_here, (2, 4)), arrived(u_here, (5, 6))]
    line_maps(*blocks, [r_here[cell, pl.ds(line, 1), :] for cell in range(2)], out, ahead, back, rows, lambda i: parts[i].start())
    for copy in copies[7:] + parts:
        copy.wait()


def second_kernel(line_ref, r, a, l, u, out, ahead, back, rows):
    line = line_ref[0]
    blocks = [lambda cell, here=here: here[cell, line] for here in (a, l, u)]
    line_maps(*blocks, [r[cell, pl.ds(line, 1), :] for cell in range(2)], out, ahead, back, rows)


def down_join_kernel(core, got, keep, chip, total, lower, a_chip, a_low):
    n = got.shape[1]

    def finish(low, high):
        matrix = product(high[0:n], low[0:n])
        put_pair(total, matrix)
        put_pair(lower, low[0:n])
        a = low[3 * n : 3 * n + 1]
        joined = high[3 * n : 3 * n + 1] + apply_full(high[0:n], a)
        chip[0:n] = matrix
        chip[n:] = jnp.broadcast_to(joined, (8, n))
        put_row(a_chip, joined)
        put_row(a_low, a)

    @pl.when(core[0] == 0)
    def _():
        finish(keep, got)

    @pl.when(core[0] == 1)
    def _():
        finish(got, keep)


def up_join_kernel(core, got, keep, chip, total, b_low, b_high, g_low, g_high, v_low, v_high):
    n = got.shape[1]

    def finish(low, high):
        matrix = product(low[2 * n : 3 * n], high[2 * n : 3 * n])
        chip[...] = matrix
        put_pair(total, matrix)
        put_pair(b_low, low[2 * n : 3 * n])
        put_pair(b_high, high[2 * n : 3 * n])
        put_pair(g_low, low[n : 2 * n])
        put_pair(g_high, high[n : 2 * n])
        put_row(v_low, low[3 * n + 1 : 3 * n + 2])
        put_row(v_high, high[3 * n + 1 : 3 * n + 2])

    @pl.when(core[0] == 0)
    def _():
        finish(keep, got)

    @pl.when(core[0] == 1)
    def _():
        finish(got, keep)


def pair_row_kernel(came, pair, row):
    n = came.shape[1]
    put_pair(pair, came[0:n])
    row[...] = came[n:]


def pair_kernel(came, pair, token):
    put_pair(pair, came[...])
    token[...] = jnp.zeros(token.shape, F32)


def total_of(refs):
    out = refs[0][0:1]
    for ref in refs[1:]:
        out = out + ref[0:1]
    return out


def step_kernel(constant, pair, *refs):
    *x, out = refs
    put_row(out, constant[0:1] + apply_pair(pair[...], total_of(x)))


def entering(before, y, x):
    return total_of(x) + apply_pair(before[...], total_of(y))


def jump_step_kernel(many, before, constant, pair, *refs):
    *x, out = refs
    put_row(out, constant[0:1] + apply_pair(pair[...], entering(before, x[:many], x[many:])))


def turn_kernel(many, before, a_low, lower, v_low, v_high, b_low, g_low, g_high, *refs):
    *x, b_chip = refs
    enter = entering(before, x[:many], x[many:])
    middle = a_low[0:1] + apply_pair(lower[...], enter)
    up = v_high[0:1] + apply_pair(g_high[...], middle)
    low = v_low[0:1] + apply_pair(g_low[...], enter)
    put_row(b_chip, low + apply_pair(b_low[...], up))


def spread_kernel(many, core, before, a_low, lower, v_high, g_high, *refs):
    *x, b_up, give, keep = refs
    enter = entering(before, x[:many], x[many:])
    middle = a_low[0:1] + apply_pair(lower[...], enter)
    put_row(b_up, v_high[0:1] + apply_pair(g_high[...], middle))
    first = core[0] == 0
    put_row(give, jnp.where(first, middle, enter))
    put_row(keep, jnp.where(first, enter, middle))


def local_kernel(size, core, here, near, give_map, keep_map, give_rows, keep_rows, got, keep, f, weights):
    n = got.shape[1]
    column = lax.broadcasted_iota(jnp.int32, (1, n), 1)
    at = here[0]
    up, down = lax.rem(at + 1, size), lax.rem(at + size - 1, size)
    even = lax.rem(at, 2) == 0
    sides = (at, jnp.where(even, up, down), jnp.where(even, down, up))
    places = [2 * side + k for side in sides for k in range(2)]
    for i, (maps, rows, enter) in enumerate(((give_map, give_rows, got), (keep_map, keep_rows, keep))):
        moved = apply_pair(maps[...], enter[0:1])
        f[i, 0:1] = rows[1:2] + moved[:, :n]
        f[i, 1:2] = rows[0:1] + moved[:, n:]
    for line in range(2):
        for k in range(6):
            row = jnp.zeros((1, n), F32)
            for face in range(4):
                inside = (column >= face * (n // 4)) & (column < (face + 1) * (n // 4))
                meets = near[line, face] == places[k]
                row = jnp.where(inside, jnp.where(meets, 1.0, 0.0), row)
            weights[line, k : k + 1] = row


def middle_kernel(many, core, before, b_up, b_high, *refs):
    *x, give, keep = refs
    enter = entering(before, x[:many], x[many:])
    middle = b_up[0:1] + apply_pair(b_high[...], enter)
    first = core[0] == 0
    put_row(give, jnp.where(first, enter, middle))
    put_row(keep, jnp.where(first, middle, enter))


def rows_exact(block, rows):
    high, low = split(rows)
    return dot(high, block) + dot(low, block)


def last_kernel(core, got, keep, f, give_map, keep_map, w, correction, own, sent):
    n = w.shape[0]
    values = []
    for i, (maps, enter) in enumerate(((give_map, got), (keep_map, keep))):
        moved = apply_pair(maps[...], enter[0:1])
        values.append((f[i, 0:1] + moved[:, n:], f[i, 1:2] - moved[:, :n]))
    index = lax.broadcasted_iota(jnp.int32, (16, n), 0)
    rows = jnp.zeros((16, n), F32)
    first = core[0] == 0
    for cell in range(2):
        given, own_row = values[0][cell], values[1][cell]
        for line, row in enumerate((jnp.where(first, own_row, given), jnp.where(first, given, own_row))):
            correction[cell, line : line + 1] = row
            rows = jnp.where(index == cell * 2 + line, jnp.broadcast_to(row, (16, n)), rows)
    traces = rows_exact(w[...], rows)[0:8]
    own[...] = traces
    width = n // 4
    column = lax.broadcasted_iota(jnp.int32, (8, n), 1)
    lower = (column < width) | ((column >= 2 * width) & (column < 3 * width))
    sent[...] = jnp.where(lower, pltpu.roll(traces, n - width, 1), pltpu.roll(traces, width, 1))


def jump_kernel(own, mine, one, other, weights, lift, residual):
    n = lift.shape[0]
    index = lax.broadcasted_iota(jnp.int32, (16, n), 0)
    rows = jnp.zeros((16, n), F32)
    for cell in range(2):
        for line in range(2):
            at = cell * 2 + line
            jump = own[at : at + 1]
            for side, source in enumerate((mine, one, other)):
                for k in range(2):
                    j = cell * 2 + k
                    jump = jump - weights[line, side * 2 + k : side * 2 + k + 1] * source[j : j + 1]
            rows = jnp.where(index == at, jnp.broadcast_to(jump, (16, n)), rows)
    out = rows_exact(lift[...], rows)
    for cell in range(2):
        residual[cell] = out[cell * 2 : cell * 2 + 2]


def chips_to(pairs):
    return [(2 * i + c, 2 * j + c) for i, j in pairs for c in range(2)]


def body(right_side, inverse_blocks, lower_blocks, upper_blocks, trace_map, lift_map, neighbours):
    n = right_side.shape[2]
    wall, tang = lax.axis_size("wall"), lax.axis_size("tang")
    chips = wall // 2
    jumps = chips // 4
    singles = chips - 2 * jumps
    core = lax.rem(lax.axis_index("wall"), 2)
    own_line = jnp.reshape(core, (1,))
    other_line = 1 - own_line
    r, a, l, u = right_side, inverse_blocks, lower_blocks, upper_blocks
    across = [(i, i ^ 1) for i in range(wall)]
    row = ((8, n), F32)
    pair = ((2 * n, n), BF16)
    joined = ((n + 8, n), F32)

    here = jnp.reshape(lax.axis_index("tang"), (1,))

    mul = 2 * n * n * n
    maps = [((3 * n + 8, n), F32), ((4 * n, n), BF16), ((4 * n, n), BF16), row]
    here_now = [(r.shape, F32)] + [(a.shape, BF16)] * 3
    give, give_ahead, give_back, give_rows, r, a, l, u = pl.pallas_call(
        first_kernel,
        out_shape=[jax.ShapeDtypeStruct(*x) for x in maps + here_now],
        in_specs=[SMEM] + [HBM] * 4,
        out_specs=[HBM] + [VMEM] * 7,
        scratch_shapes=[
            pltpu.VMEM((3 * n + 8, n), F32), pltpu.SemaphoreType.DMA((13,)), pltpu.SemaphoreType.DMA((3,))
        ],
        compiler_params=pltpu.CompilerParams(vmem_limit_bytes=WHOLE),
        cost_estimate=pl.CostEstimate(flops=13 * mul, bytes_accessed=0, transcendentals=0),
        name="first",
    )(other_line, r, a, l, u)
    got = lax.ppermute(give, "wall", across)
    keep, keep_ahead, keep_back, keep_rows = call(
        second_kernel, maps, own_line, r, a, l, u, scalars=1, flops=13 * mul, name="second"
    )
    chip_f, total, lower, a_chip, a_low = call(
        down_join_kernel, [joined, pair, pair, row, row], own_line, got, keep,
        scalars=1, flops=3 * mul, name="down_join",
    )
    chip_b, back, b_low, b_high, g_low, g_high, v_low, v_high = call(
        up_join_kernel, [((n, n), F32)] + [pair] * 5 + [row] * 2, own_line, got, keep,
        scalars=1, flops=3 * mul, name="up_join", after=(a_chip,),
    )
    moved_b = lax.ppermute(chip_b, "wall", chips_to([(k, k - 1) for k in range(chips - 2, 0, -2)]))

    moved_f = lax.ppermute(
        chip_f, "wall", chips_to([(k, k + 1) for k in range(singles, chips, 2)])
    )
    x, y = [], []
    out = a_chip
    for k in range(1, singles):
        x.append(lax.ppermute(out, "wall", chips_to([(k - 1, k)])))
        (out,) = call(step_kernel, [row], a_chip, total, *x, flops=mul // 100, name="step")
    pre, pre_row = call(pair_row_kernel, [pair, row], moved_f, flops=mul // 10, name="pre")
    for k in range(jumps):
        last = singles + 2 * k - 1
        y.append(lax.ppermute(out, "wall", chips_to([(last, last + 2)])))
        if k == jumps - 1:
            side = lax.ppermute(
                out, "wall", chips_to([(singles + 2 * j - 1, singles + 2 * j) for j in range(jumps)])
            )
        else:
            (out,) = call(
                functools.partial(jump_step_kernel, k + 1), [row], pre, a_chip, total, *y, *x, pre_row,
                flops=mul // 50, name="jump_step",
            )
    x = [*x, side, pre_row]
    entry, token = call(pair_kernel, [pair, row], moved_b, flops=mul // 10, name="entry")
    (b_chip,) = call(
        functools.partial(turn_kernel, jumps), [row],
        pre, a_low, lower, v_low, v_high, b_low, g_low, g_high, *y, *x,
        flops=mul // 50, name="turn", after=(token,),
    )

    odd = list(range(chips - 1, 0, -2))
    z = []
    out = b_chip
    waits = ()
    for k in odd[1:]:
        z.append(lax.ppermute(out, "wall", chips_to([(k + 2, k)])))
        if len(z) == 1:
            sent = lax.ppermute(b_chip, "wall", chips_to([(j, j - 1) for j in range(chips - 2, 0, -2)]))
        if k == 1:
            done = out
            upper_ends = lax.ppermute(out, "wall", chips_to([(j, j - 1) for j in odd[:-1]]))
            b_up, give, keep = call(
                functools.partial(spread_kernel, jumps), [row] * 3, own_line, pre, a_low, lower, v_high, g_high, *y, *x,
                scalars=1, flops=mul // 50, name="spread",
            )
            got = lax.ppermute(give, "wall", across)
            forward, weights = call(
                functools.partial(local_kernel, tang), [((2, 2, n), F32), ((2, 8, n), F32)],
            own_line, here, neighbours, give_ahead, keep_ahead, give_rows, keep_rows, got, keep,
                scalars=3, flops=mul // 20, name="local",
            )
            waits = (weights,)
        (out,) = call(
            functools.partial(jump_step_kernel, len(z)), [row], entry, b_chip, back, *z, sent,
            flops=mul // 50, name="back_step", after=waits,
        )
    ends = lax.ppermute(out, "wall", chips_to([(1, 0)]))

    give, keep = call(
        functools.partial(middle_kernel, len(z)), [row] * 2, own_line, entry, b_up, b_high, *z, sent, ends, upper_ends,
        scalars=1, flops=mul // 100, name="middle", after=(forward,),
    )
    got = lax.ppermute(give, "wall", across)
    correction, traces, sent = call(
        last_kernel, [((2, 2, n), F32), row, row], own_line, got, keep, forward, give_back, keep_back, trace_map,
        scalars=1, flops=mul // 20, name="last",
    )
    first = [(i, i + 1) for i in range(0, tang, 2)]
    second = [(i, (i + 1) % tang) for i in range(1, tang, 2)]
    from_near = lax.ppermute(sent, "tang", first + [(j, i) for i, j in first])
    from_far = lax.ppermute(sent, "tang", second + [(j, i) for i, j in second])
    (residual,) = call(
        jump_kernel, [((2, 2, n), F32)], traces, sent, from_near, from_far, weights, lift_map,
        flops=mul // 50, name="jump",
    )
    return correction, residual


def solution(mesh):
    in_specs = (
        P("wall", "tang", None),
        P("wall", "tang", None, None),
        P("wall", "tang", None, None),
        P("wall", "tang", None, None),
        P(),
        P(),
        P("tang", None),
    )
    out_specs = (P("wall", "tang", None), P("wall", "tang", None))
    return jax.shard_map(body, mesh=mesh, in_specs=in_specs, out_specs=out_specs, check_vma=False)
```

```python
import functools

import jax
import jax.numpy as jnp
from jax import lax
from jax.experimental import pallas as pl
from jax.experimental.pallas import tpu as pltpu
from jax.sharding import PartitionSpec as P

F32 = jnp.float32
BF16 = jnp.bfloat16
NN = (((1,), (0,)), ((), ()))
NT = (((1,), (1,)), ((), ()))
VMEM = pl.BlockSpec(memory_space=pltpu.VMEM)
HBM = pl.BlockSpec(memory_space=pltpu.HBM)
SMEM = pl.BlockSpec(memory_space=pltpu.SMEM)
LIMIT = 16 * 1024 * 1024
WHOLE = 48 * 1024 * 1024


def dot(a, b, dims=NN):
    return lax.dot_general(a, b, dims, preferred_element_type=F32)


def split(x):
    high = x.astype(BF16)
    return high, (x - high.astype(F32)).astype(BF16)


def product(a, b):
    a_high, a_low = split(a)
    b_high, b_low = split(b)
    return dot(a_high, b_high) + dot(a_high, b_low) + dot(a_low, b_high)


def stacked(row):
    high, low = split(row)
    index = lax.broadcasted_iota(jnp.int32, (16, row.shape[1]), 0)
    zero = jnp.zeros((16, row.shape[1]), F32)
    high = jnp.broadcast_to(high.astype(F32), zero.shape)
    low = jnp.broadcast_to(low.astype(F32), zero.shape)
    return jnp.where(index == 0, high, jnp.where(index == 1, low, zero)).astype(BF16)


def apply_exact(block, row):
    out = dot(stacked(row), block, NT)
    return out[0:1] + out[1:2]


def apply_pair(pair, row):
    n = pair.shape[0] // 2
    out = dot(stacked(row), pair, NT)
    return out[0:1, :n] + out[1:2, :n] + out[0:1, n:]


def apply_full(matrix, row):
    high, low = split(matrix)
    rows = stacked(row)
    main = dot(rows, high, NT)
    rest = dot(rows, low, NT)
    return main[0:1] + main[1:2] + rest[0:1]


def put_pair(ref, matrix):
    n = matrix.shape[0]
    high, low = split(matrix)
    ref[0:n] = high
    ref[n:] = low


def put_row(ref, row):
    ref[...] = jnp.broadcast_to(row, ref.shape)


def call(kernel, outs, *args, scalars=0, flops=0, name=None, after=()):
    count = len(args)
    operands = list(args) + list(after)

    def inner(*refs):
        kernel(*refs[:count], *refs[len(operands) :])

    return pl.pallas_call(
        inner,
        out_shape=[jax.ShapeDtypeStruct(s, t) for s, t in outs],
        in_specs=[SMEM] * scalars + [VMEM] * (len(operands) - scalars),
        out_specs=[VMEM] * len(outs),
        compiler_params=pltpu.CompilerParams(vmem_limit_bytes=LIMIT),
        cost_estimate=pl.CostEstimate(flops=flops, bytes_accessed=0, transcendentals=0),
        name=name,
    )(*operands)


def line_maps(a, l, u, r, out, ahead, back, rows, sent=lambda part: None):
    n = r[0].shape[1]
    a0, l0 = a(0), l(0)
    first = dot(a0, l0)
    x = apply_exact(a0, r[0])
    a1, l1 = a(1), l(1)
    up = product(dot(a1, l1), first)
    out[0:n] = up
    sent(0)
    y = apply_exact(a1, r[1] - apply_exact(l1, x))
    u0 = u(0)
    near = dot(a0, u0)
    turn = -(first + product(near, up))
    out[n : 2 * n] = turn
    sent(1)
    x = x - apply_exact(a0, apply_exact(u0, y))
    far = dot(a1, u(1))
    down = product(near, far)
    out[2 * n : 3 * n] = down
    index = lax.broadcasted_iota(jnp.int32, (8, n), 0)
    both = jnp.where(index == 0, jnp.broadcast_to(y, (8, n)), jnp.broadcast_to(x, (8, n)))
    out[3 * n :] = both
    sent(2)
    rows[...] = both
    for ref, parts in ((ahead, (turn, up)), (back, (far, down))):
        for i, part in enumerate(parts):
            high, low = split(part)
            ref[i * n : (i + 1) * n] = high
            ref[(2 + i) * n : (3 + i) * n] = low


def first_kernel(line_ref, r, a, l, u, given, ahead, back, rows, r_here, a_here, l_here, u_here, out, sems, out_sems):
    line = line_ref[0]
    copies = [pltpu.make_async_copy(r, r_here, sems.at[0])]
    for at in (line, 1 - line):
        for cell, source, here in (
            (0, a, a_here), (0, l, l_here), (1, a, a_here), (1, l, l_here), (0, u, u_here), (1, u, u_here)
        ):
            copies.append(pltpu.make_async_copy(source.at[cell, at], here.at[cell, at], sems.at[len(copies)]))
    for copy in copies[:7]:
        copy.start()

    def arrived(here, place):
        def get(cell):
            copies[place[cell]].wait()
            if place[cell] == 5:
                for copy in copies[7:]:
                    copy.start()
            return here[cell, line]

        return get

    n = r.shape[2]
    parts = []
    for i, (start, size) in enumerate(((0, n), (n, n), (2 * n, n + 8))):
        at = pl.ds(start, size)
        parts.append(pltpu.make_async_copy(out.at[at], given.at[at], out_sems.at[i]))

    copies[0].wait()
    blocks = [arrived(a_here, (1, 3)), arrived(l_here, (2, 4)), arrived(u_here, (5, 6))]
    line_maps(*blocks, [r_here[cell, pl.ds(line, 1), :] for cell in range(2)], out, ahead, back, rows, lambda i: parts[i].start())
    for copy in copies[7:] + parts:
        copy.wait()


def second_kernel(line_ref, r, a, l, u, out, ahead, back, rows):
    line = line_ref[0]
    blocks = [lambda cell, here=here: here[cell, line] for here in (a, l, u)]
    line_maps(*blocks, [r[cell, pl.ds(line, 1), :] for cell in range(2)], out, ahead, back, rows)


def down_join_kernel(core, got, keep, chip, total, lower, a_chip, a_low):
    n = got.shape[1]

    def finish(low, high):
        matrix = product(high[0:n], low[0:n])
        put_pair(total, matrix)
        put_pair(lower, low[0:n])
        a = low[3 * n : 3 * n + 1]
        joined = high[3 * n : 3 * n + 1] + apply_full(high[0:n], a)
        chip[0:n] = matrix
        chip[n:] = jnp.broadcast_to(joined, (8, n))
        put_row(a_chip, joined)
        put_row(a_low, a)

    @pl.when(core[0] == 0)
    def _():
        finish(keep, got)

    @pl.when(core[0] == 1)
    def _():
        finish(got, keep)


def up_join_kernel(core, got, keep, chip, total, b_low, b_high, g_low, g_high, v_low, v_high):
    n = got.shape[1]

    def finish(low, high):
        matrix = product(low[2 * n : 3 * n], high[2 * n : 3 * n])
        chip[...] = matrix
        put_pair(total, matrix)
        put_pair(b_low, low[2 * n : 3 * n])
        put_pair(b_high, high[2 * n : 3 * n])
        put_pair(g_low, low[n : 2 * n])
        put_pair(g_high, high[n : 2 * n])
        put_row(v_low, low[3 * n + 1 : 3 * n + 2])
        put_row(v_high, high[3 * n + 1 : 3 * n + 2])

    @pl.when(core[0] == 0)
    def _():
        finish(keep, got)

    @pl.when(core[0] == 1)
    def _():
        finish(got, keep)


def pair_row_kernel(came, pair, row):
    n = came.shape[1]
    put_pair(pair, came[0:n])
    row[...] = came[n:]


def pair_kernel(came, pair, token):
    put_pair(pair, came[...])
    token[...] = jnp.zeros(token.shape, F32)


def total_of(refs):
    out = refs[0][0:1]
    for ref in refs[1:]:
        out = out + ref[0:1]
    return out


def step_kernel(constant, pair, *refs):
    *x, out = refs
    put_row(out, constant[0:1] + apply_pair(pair[...], total_of(x)))


def entering(before, y, x):
    return total_of(x) + apply_pair(before[...], total_of(y))


def jump_step_kernel(many, before, constant, pair, *refs):
    *x, out, come = refs
    enter = entering(before, x[:many], x[many:])
    put_row(out, constant[0:1] + apply_pair(pair[...], enter))
    put_row(come, enter)


def turn_kernel(many, before, a_low, lower, v_low, v_high, b_low, g_low, g_high, *refs):
    *x, b_chip = refs
    enter = entering(before, x[:many], x[many:])
    middle = a_low[0:1] + apply_pair(lower[...], enter)
    up = v_high[0:1] + apply_pair(g_high[...], middle)
    low = v_low[0:1] + apply_pair(g_low[...], enter)
    put_row(b_chip, low + apply_pair(b_low[...], up))


def spread_kernel(many, core, before, a_low, lower, v_high, g_high, *refs):
    *x, b_up, give, keep = refs
    enter = entering(before, x[:many], x[many:])
    middle = a_low[0:1] + apply_pair(lower[...], enter)
    put_row(b_up, v_high[0:1] + apply_pair(g_high[...], middle))
    first = core[0] == 0
    put_row(give, jnp.where(first, middle, enter))
    put_row(keep, jnp.where(first, enter, middle))


def local_kernel(size, core, here, near, give_map, keep_map, give_rows, keep_rows, got, keep, f, weights):
    n = got.shape[1]
    column = lax.broadcasted_iota(jnp.int32, (1, n), 1)
    at = here[0]
    up, down = lax.rem(at + 1, size), lax.rem(at + size - 1, size)
    even = lax.rem(at, 2) == 0
    sides = (at, jnp.where(even, up, down), jnp.where(even, down, up))
    places = [2 * side + k for side in sides for k in range(2)]
    for i, (maps, rows, enter) in enumerate(((give_map, give_rows, got), (keep_map, keep_rows, keep))):
        moved = apply_pair(maps[...], enter[0:1])
        f[i, 0:1] = rows[1:2] + moved[:, :n]
        f[i, 1:2] = rows[0:1] + moved[:, n:]
    for line in range(2):
        for k in range(6):
            row = jnp.zeros((1, n), F32)
            for face in range(4):
                inside = (column >= face * (n // 4)) & (column < (face + 1) * (n // 4))
                meets = near[line, face] == places[k]
                row = jnp.where(inside, jnp.where(meets, 1.0, 0.0), row)
            weights[line, k : k + 1] = row


def middle_kernel(core, b_up, b_high, *refs):
    *x, give, keep = refs
    enter = total_of(x)
    middle = b_up[0:1] + apply_pair(b_high[...], enter)
    first = core[0] == 0
    put_row(give, jnp.where(first, enter, middle))
    put_row(keep, jnp.where(first, middle, enter))


def rows_exact(block, rows):
    high, low = split(rows)
    return dot(high, block) + dot(low, block)


def last_kernel(core, got, keep, f, give_map, keep_map, w, correction, own, sent):
    n = w.shape[0]
    values = []
    for i, (maps, enter) in enumerate(((give_map, got), (keep_map, keep))):
        moved = apply_pair(maps[...], enter[0:1])
        values.append((f[i, 0:1] + moved[:, n:], f[i, 1:2] - moved[:, :n]))
    index = lax.broadcasted_iota(jnp.int32, (16, n), 0)
    rows = jnp.zeros((16, n), F32)
    first = core[0] == 0
    for cell in range(2):
        given, own_row = values[0][cell], values[1][cell]
        for line, row in enumerate((jnp.where(first, own_row, given), jnp.where(first, given, own_row))):
            correction[cell, line : line + 1] = row
            rows = jnp.where(index == cell * 2 + line, jnp.broadcast_to(row, (16, n)), rows)
    traces = rows_exact(w[...], rows)[0:8]
    own[...] = traces
    width = n // 4
    column = lax.broadcasted_iota(jnp.int32, (8, n), 1)
    lower = (column < width) | ((column >= 2 * width) & (column < 3 * width))
    sent[...] = jnp.where(lower, pltpu.roll(traces, n - width, 1), pltpu.roll(traces, width, 1))


def jump_kernel(own, mine, one, other, weights, lift, residual):
    n = lift.shape[0]
    index = lax.broadcasted_iota(jnp.int32, (16, n), 0)
    rows = jnp.zeros((16, n), F32)
    for cell in range(2):
        for line in range(2):
            at = cell * 2 + line
            jump = own[at : at + 1]
            for side, source in enumerate((mine, one, other)):
                for k in range(2):
                    j = cell * 2 + k
                    jump = jump - weights[line, side * 2 + k : side * 2 + k + 1] * source[j : j + 1]
            rows = jnp.where(index == at, jnp.broadcast_to(jump, (16, n)), rows)
    out = rows_exact(lift[...], rows)
    for cell in range(2):
        residual[cell] = out[cell * 2 : cell * 2 + 2]


def chips_to(pairs):
    return [(2 * i + c, 2 * j + c) for i, j in pairs for c in range(2)]


def body(right_side, inverse_blocks, lower_blocks, upper_blocks, trace_map, lift_map, neighbours):
    n = right_side.shape[2]
    wall, tang = lax.axis_size("wall"), lax.axis_size("tang")
    chips = wall // 2
    jumps = chips // 4
    singles = chips - 2 * jumps
    core = lax.rem(lax.axis_index("wall"), 2)
    own_line = jnp.reshape(core, (1,))
    other_line = 1 - own_line
    r, a, l, u = right_side, inverse_blocks, lower_blocks, upper_blocks
    across = [(i, i ^ 1) for i in range(wall)]
    row = ((8, n), F32)
    pair = ((2 * n, n), BF16)
    joined = ((n + 8, n), F32)

    here = jnp.reshape(lax.axis_index("tang"), (1,))

    mul = 2 * n * n * n
    maps = [((3 * n + 8, n), F32), ((4 * n, n), BF16), ((4 * n, n), BF16), row]
    here_now = [(r.shape, F32)] + [(a.shape, BF16)] * 3
    give, give_ahead, give_back, give_rows, r, a, l, u = pl.pallas_call(
        first_kernel,
        out_shape=[jax.ShapeDtypeStruct(*x) for x in maps + here_now],
        in_specs=[SMEM] + [HBM] * 4,
        out_specs=[HBM] + [VMEM] * 7,
        scratch_shapes=[
            pltpu.VMEM((3 * n + 8, n), F32), pltpu.SemaphoreType.DMA((13,)), pltpu.SemaphoreType.DMA((3,))
        ],
        compiler_params=pltpu.CompilerParams(vmem_limit_bytes=WHOLE),
        cost_estimate=pl.CostEstimate(flops=13 * mul, bytes_accessed=0, transcendentals=0),
        name="first",
    )(other_line, r, a, l, u)
    got = lax.ppermute(give, "wall", across)
    keep, keep_ahead, keep_back, keep_rows = call(
        second_kernel, maps, own_line, r, a, l, u, scalars=1, flops=13 * mul, name="second"
    )
    chip_f, total, lower, a_chip, a_low = call(
        down_join_kernel, [joined, pair, pair, row, row], own_line, got, keep,
        scalars=1, flops=3 * mul, name="down_join",
    )
    chip_b, back, b_low, b_high, g_low, g_high, v_low, v_high = call(
        up_join_kernel, [((n, n), F32)] + [pair] * 5 + [row] * 2, own_line, got, keep,
        scalars=1, flops=3 * mul, name="up_join", after=(a_chip,),
    )
    moved_b = lax.ppermute(chip_b, "wall", chips_to([(k, k - 1) for k in range(chips - 2, 0, -2)]))

    moved_f = lax.ppermute(
        chip_f, "wall", chips_to([(k, k + 1) for k in range(singles, chips, 2)])
    )
    x, y = [], []
    out = a_chip
    for k in range(1, singles):
        x.append(lax.ppermute(out, "wall", chips_to([(k - 1, k)])))
        (out,) = call(step_kernel, [row], a_chip, total, *x, flops=mul // 100, name="step")
    pre, pre_row = call(pair_row_kernel, [pair, row], moved_f, flops=mul // 10, name="pre")
    for k in range(jumps):
        last = singles + 2 * k - 1
        y.append(lax.ppermute(out, "wall", chips_to([(last, last + 2)])))
        if k == jumps - 1:
            side = lax.ppermute(
                out, "wall", chips_to([(singles + 2 * j - 1, singles + 2 * j) for j in range(jumps)])
            )
        else:
            out, _ = call(
                functools.partial(jump_step_kernel, k + 1), [row] * 2, pre, a_chip, total, *y, *x, pre_row,
                flops=mul // 50, name="jump_step",
            )
    x = [*x, side, pre_row]
    entry, token = call(pair_kernel, [pair, row], moved_b, flops=mul // 10, name="entry")
    (b_chip,) = call(
        functools.partial(turn_kernel, jumps), [row],
        pre, a_low, lower, v_low, v_high, b_low, g_low, g_high, *y, *x,
        flops=mul // 50, name="turn", after=(token,),
    )

    odd = list(range(chips - 1, 0, -2))
    z = []
    out = b_chip
    waits = ()
    for k in odd[1:]:
        z.append(lax.ppermute(out, "wall", chips_to([(k + 2, k)])))
        if len(z) == 1:
            sent = lax.ppermute(b_chip, "wall", chips_to([(j, j - 1) for j in range(chips - 2, 0, -2)]))
        if k == 1:
            done = out
            upper_ends = lax.ppermute(out, "wall", chips_to([(j, j - 1) for j in odd[:-1]]))
            b_up, give, keep = call(
                functools.partial(spread_kernel, jumps), [row] * 3, own_line, pre, a_low, lower, v_high, g_high, *y, *x,
                scalars=1, flops=mul // 50, name="spread",
            )
            got = lax.ppermute(give, "wall", across)
            forward, weights = call(
                functools.partial(local_kernel, tang), [((2, 2, n), F32), ((2, 8, n), F32)],
            own_line, here, neighbours, give_ahead, keep_ahead, give_rows, keep_rows, got, keep,
                scalars=3, flops=mul // 20, name="local",
            )
            waits = (weights,)
        out, come = call(
            functools.partial(jump_step_kernel, len(z)), [row] * 2, entry, b_chip, back, *z, sent,
            flops=mul // 50, name="back_step", after=waits,
        )
    ends = lax.ppermute(out, "wall", chips_to([(1, 0)]))

    give, keep = call(
        middle_kernel, [row] * 2, own_line, b_up, b_high, come, ends, upper_ends,
        scalars=1, flops=mul // 100, name="middle", after=(forward,),
    )
    got = lax.ppermute(give, "wall", across)
    correction, traces, sent = call(
        last_kernel, [((2, 2, n), F32), row, row], own_line, got, keep, forward, give_back, keep_back, trace_map,
        scalars=1, flops=mul // 20, name="last",
    )
    first = [(i, i + 1) for i in range(0, tang, 2)]
    second = [(i, (i + 1) % tang) for i in range(1, tang, 2)]
    from_near = lax.ppermute(sent, "tang", first + [(j, i) for i, j in first])
    from_far = lax.ppermute(sent, "tang", second + [(j, i) for i, j in second])
    (residual,) = call(
        jump_kernel, [((2, 2, n), F32)], traces, sent, from_near, from_far, weights, lift_map,
        flops=mul // 50, name="jump",
    )
    return correction, residual


def solution(mesh):
    in_specs = (
        P("wall", "tang", None),
        P("wall", "tang", None, None),
        P("wall", "tang", None, None),
        P("wall", "tang", None, None),
        P(),
        P(),
        P("tang", None),
    )
    out_specs = (P("wall", "tang", None), P("wall", "tang", None))
    return jax.shard_map(body, mesh=mesh, in_specs=in_specs, out_specs=out_specs, check_vma=False)
```
